32 devices in a mesh: chan: 8 (over z, core), win: 4 (over y, x).
Axes of the slice: x: 2, y: 2, z: 4, core: 2. Of those that a mesh axis runs over, the one named last changes fastest.
Arguments:
- series: bfloat16 [32, 2048, 1500], P('win', 'chan'), may hold values from -1700 to 1700
- validity: int32 [32, 2048], P('win', 'chan'), may hold values from 0 to 1, as said below
Outputs:
- source_gathers: float32 [2048, 8, 4, 64, 128], P('chan', None, 'win')
The draws below stay inside these ranges and needn't reach their ends.
Inputs may be any that keep to these rules, and one draw needn't show every extreme that they name: `validity`: a channel flagged dead is 0 in every window.
All inputs are finite; a program needn't handle non-finite values.
Results may differ from the reference program's by a relative error of at most 0.0037.
Values may be sent and summed in bfloat16 or wider, within the bound.
A program may use at most 448 MiB of HBM per device.

```python
import math
import jax
import jax.numpy as jnp
from jax import lax

CHANNELS = 2048
SAMPLES = 1500
BINS = 128
LAGS = 128
SOURCES = 2048
WINDOWS = 32
CH_SUB = 64
N_CHAN = 8
N_WIN = 4


def draw_series(key, part):
    subkeys = jax.random.split(key, 3)
    full_shape = (WINDOWS, CHANNELS, SAMPLES)
    noise_base = jnp.clip(jax.random.normal(subkeys[0], full_shape, jnp.float32), -6.0, 6.0)
    log_top = math.log(10.0)
    chan_scale = jnp.exp(jax.random.uniform(subkeys[1], (1, CHANNELS, 1), jnp.float32, 0.0, log_top))
    window_scale = jnp.exp(jax.random.uniform(subkeys[2], (WINDOWS, 1, 1), jnp.float32, 0.0, log_top))
    return (noise_base * chan_scale * window_scale).astype(jnp.bfloat16)


def draw_validity(key, part):
    subkeys = jax.random.split(key, 2)
    dead_channel = jax.random.randint(subkeys[0], (1, CHANNELS), 0, 16) == 0
    glitch = jax.random.randint(subkeys[1], (WINDOWS, CHANNELS), 0, 100) < 15
    return jnp.where(dead_channel | glitch, 0, 1).astype(jnp.int32)


def setup_inputs(seed: int = 0) -> dict:
    keys = jax.random.split(jax.random.key(seed), 3)
    return {
        "series": draw_series(jax.random.fold_in(keys[2], 71), 0),
        "validity": draw_validity(jax.random.fold_in(keys[2], 71), 0),
    }


lowest_bin = 6

def build_tables():
    sample_idx = jnp.arange(SAMPLES, dtype=jnp.int32)
    bin_idx = jnp.arange(BINS, dtype=jnp.int32) + lowest_bin
    phase_index = sample_idx[:, None] * bin_idx[None, :] % SAMPLES
    phase_angle = phase_index.astype(jnp.float32) * (2.0 * math.pi / SAMPLES)
    hann_taper = 0.5 - 0.5 * jnp.cos(sample_idx.astype(jnp.float32) * (2.0 * math.pi / SAMPLES))
    taper_table = jnp.concatenate([hann_taper[:, None] * jnp.cos(phase_angle), -hann_taper[:, None] * jnp.sin(phase_angle)], axis=1).astype(jnp.bfloat16)
    lag_idx = jnp.arange(LAGS, dtype=jnp.int32) - LAGS // 2
    lag_index = bin_idx[:, None] * lag_idx[None, :] % SAMPLES
    lag_angle = lag_index.astype(jnp.float32) * (2.0 * math.pi / SAMPLES)
    inverse = jnp.concatenate([jnp.cos(lag_angle), -jnp.sin(lag_angle)], axis=0)
    return (taper_table, inverse)

def reference(series, validity):
    taper_table, inverse = build_tables()
    stride = CHANNELS // SOURCES
    flag_float = validity.astype(jnp.float32)
    spectra = jnp.dot(series.reshape(WINDOWS * CHANNELS, SAMPLES), taper_table, preferred_element_type=jnp.float32)
    spectra = spectra.reshape(WINDOWS, CHANNELS, 2 * BINS)
    energy = lax.optimization_barrier(jnp.mean(spectra * spectra, axis=-1, keepdims=True))
    rounded = (spectra * lax.rsqrt(energy + 1e-06) * flag_float[..., None]).astype(jnp.bfloat16)
    whitened = lax.optimization_barrier(rounded).astype(jnp.float32)
    recv_real = whitened[..., :BINS]
    recv_imag = whitened[..., BINS:]
    block_size = SOURCES // 16
    sources = whitened[:, ::stride].reshape(WINDOWS, 16, block_size, 2 * BINS).transpose(1, 0, 2, 3)

    def one_block(source_block):
        src_real = source_block[..., :BINS]
        src_imag = source_block[..., BINS:]
        in_phase = jnp.einsum('wsk,wik->sik', src_real, recv_real) + jnp.einsum('wsk,wik->sik', src_imag, recv_imag)
        quadrature = jnp.einsum('wsk,wik->sik', src_real, recv_imag) - jnp.einsum('wsk,wik->sik', src_imag, recv_real)
        joined = jnp.concatenate([in_phase, quadrature], axis=-1)
        return jnp.einsum('sik,kt->sit', joined, inverse, precision=lax.Precision.HIGHEST)
    correlation = lax.map(one_block, sources).reshape(SOURCES, CHANNELS, LAGS)
    pair_count = jnp.einsum('ws,wi->si', flag_float[:, ::stride], flag_float, precision=lax.Precision.HIGHEST)
    result = correlation / jnp.maximum(pair_count, 1.0)[..., None]
    return result.reshape(SOURCES, N_CHAN, N_WIN, CH_SUB, LAGS)
```

```python
import functools
import math

import jax
import jax.numpy as jnp
import ml_dtypes
import numpy as np
from jax import lax
from jax.experimental import pallas as pl
from jax.experimental.pallas import tpu as pltpu
from jax.sharding import PartitionSpec as P

BINS = 128
LAGS = 128
LOWEST_BIN = 6


def build_tables(samples):
    t = np.arange(samples)
    k = np.arange(BINS) + LOWEST_BIN
    step = 2.0 * math.pi / samples
    angle = (t[:, None] * k[None, :] % samples) * step
    hann = 0.5 - 0.5 * np.cos(t * step)
    taper = np.concatenate(
        [hann[:, None] * np.cos(angle), -hann[:, None] * np.sin(angle)], axis=1
    )
    lag = np.arange(LAGS) - LAGS // 2
    lag_angle = (k[:, None] * lag[None, :] % samples) * step
    inverse = np.concatenate([np.cos(lag_angle), -np.sin(lag_angle)], axis=0)
    to_half = lambda x: x.astype(np.float32).astype(ml_dtypes.bfloat16)
    return to_half(taper), to_half(inverse)


def pair_kernel(src_ref, recv_ref, scale_ref, inv_ref, out_ref, cross):
    bins, _, sc, depth = src_ref.shape
    ti = recv_ref.shape[2]
    slot = out_ref.shape[3]
    halves = ti // 128

    def bin_step(k, carry):
        r = recv_ref[k]
        l = src_ref[k].reshape(2 * sc, depth)
        x = jnp.dot(l, r, preferred_element_type=jnp.float32)
        for h in range(halves):
            part = x[:, h * 128 : (h + 1) * 128]
            cross[h, pl.ds(pl.multiple_of(k * sc, sc), sc), :] = part[:sc]
            cross[h, pl.ds(pl.multiple_of((bins + k) * sc, sc), sc), :] = part[sc:]
        return carry

    lax.fori_loop(0, bins, bin_step, 0, unroll=8)

    inv = inv_ref[...]
    per = 128 // slot

    def source_step(s, carry):
        for h in range(halves):
            x = cross[h, pl.ds(s, 2 * bins, stride=sc), :]
            x = x * scale_ref[s][:, h * 128 : (h + 1) * 128]
            y = lax.dot_general(
                x.astype(jnp.bfloat16),
                inv,
                (((0,), (0,)), ((), ())),
                preferred_element_type=jnp.float32,
            )
            out_ref[s, h * per : (h + 1) * per, 0] = y.reshape(per, slot, LAGS)
        return carry

    lax.fori_loop(0, sc, source_step, 0, unroll=4)


def pair_block(src, recv, scale, inverse, slot):
    bins, _, sources, depth = src.shape
    receivers = recv.shape[2]
    sc = min(64, sources)
    ti = min(256, receivers)
    return pl.pallas_call(
        pair_kernel,
        grid=(receivers // ti, sources // sc),
        in_specs=[
            pl.BlockSpec((bins, 2, sc, depth), lambda i, s: (0, 0, s, 0)),
            pl.BlockSpec((bins, depth, ti), lambda i, s: (0, 0, i)),
            pl.BlockSpec((sc, 1, ti), lambda i, s: (s, 0, i)),
            pl.BlockSpec((2 * bins, LAGS), lambda i, s: (0, 0)),
        ],
        out_specs=pl.BlockSpec(
            (sc, ti // slot, 1, slot, LAGS), lambda i, s: (s, i, 0, 0, 0)
        ),
        out_shape=jax.ShapeDtypeStruct(
            (sources, receivers // slot, 1, slot, LAGS), jnp.float32
        ),
        scratch_shapes=[pltpu.VMEM((ti // 128, 2 * bins * sc, 128), jnp.float32)],
        compiler_params=pltpu.CompilerParams(vmem_limit_bytes=58 * 1024 * 1024),
        cost_estimate=pl.CostEstimate(
            flops=2 * sources * receivers * 2 * bins * (depth + LAGS),
            bytes_accessed=sources * receivers * LAGS * 4,
            transcendentals=0,
        ),
        name="pairs",
    )(src, recv, scale[:, None, :], inverse)


def on_device(series, validity):
    win_rows, channels, samples = series.shape
    taper, inverse = build_tables(samples)
    spectra = jnp.dot(
        series.reshape(win_rows * channels, samples),
        jnp.asarray(taper),
        preferred_element_type=jnp.float32,
    ).reshape(win_rows, channels, 2 * BINS)
    energy = jnp.mean(spectra * spectra, axis=-1, keepdims=True)
    flag_float = validity.astype(jnp.float32)
    whitened = (spectra * lax.rsqrt(energy + 1e-06) * flag_float[..., None]).astype(jnp.bfloat16)
    flags = validity.astype(jnp.bfloat16)

    blocks = lax.axis_size("chan")
    slots = lax.axis_size("win")
    slot = channels // slots
    v = lax.axis_index("win")

    src = lax.all_gather(whitened, "win", axis=0, tiled=True)
    windows = src.shape[0]
    own = lax.dynamic_slice_in_dim(src, v * slot, slot, axis=1)
    recv = lax.all_gather(own, "chan", axis=1, tiled=True)
    src_flags = lax.all_gather(flags, "win", axis=0, tiled=True)
    own_flags = lax.dynamic_slice_in_dim(src_flags, v * slot, slot, axis=1)
    recv_flags = lax.all_gather(own_flags, "chan", axis=1, tiled=True)
    count = jnp.einsum("ws,wi->si", src_flags, recv_flags, preferred_element_type=jnp.float32)
    scale = 1.0 / jnp.maximum(count, 1.0)

    s4 = src.reshape(windows, channels, 2, BINS).transpose(3, 2, 1, 0)
    real, imag = s4[:, 0], s4[:, 1]
    src_l = jnp.stack(
        [jnp.concatenate([real, imag], -1), jnp.concatenate([-imag, real], -1)], axis=1
    )
    receivers = blocks * slot
    recv_r = recv.reshape(windows, receivers, 2, BINS).transpose(3, 2, 0, 1)
    recv_r = recv_r.reshape(BINS, 2 * windows, receivers)
    return pair_block(src_l, recv_r, scale, jnp.asarray(inverse), slot)


def solution(mesh):
    return jax.shard_map(
        on_device,
        mesh=mesh,
        in_specs=(P("win", "chan", None), P("win", "chan")),
        out_specs=P("chan", None, "win", None, None),
        check_vma=False,
    )
```

```python
import functools
import math

import jax
import jax.numpy as jnp
import ml_dtypes
import numpy as np
from jax import lax
from jax.experimental import pallas as pl
from jax.experimental.pallas import tpu as pltpu
from jax.sharding import PartitionSpec as P

BINS = 128
LAGS = 128
LOWEST_BIN = 6


def build_tables(samples):
    t = np.arange(samples)
    k = np.arange(BINS) + LOWEST_BIN
    step = 2.0 * math.pi / samples
    angle = (t[:, None] * k[None, :] % samples) * step
    hann = 0.5 - 0.5 * np.cos(t * step)
    taper = np.concatenate(
        [hann[:, None] * np.cos(angle), -hann[:, None] * np.sin(angle)], axis=1
    )
    lag = np.arange(LAGS) - LAGS // 2
    lag_angle = (k[:, None] * lag[None, :] % samples) * step
    inverse = np.concatenate([np.cos(lag_angle), -np.sin(lag_angle)], axis=0)
    to_half = lambda x: x.astype(np.float32).astype(ml_dtypes.bfloat16)
    return to_half(taper), to_half(inverse)


def pair_kernel(src_ref, recv_ref, scale_ref, inv_ref, out_ref, cross):
    bins, _, sc, depth = src_ref.shape
    ti = recv_ref.shape[2]
    slot = out_ref.shape[3]
    halves = ti // 128

    def bin_step(k, carry):
        r = recv_ref[k]
        l = src_ref[k].reshape(2 * sc, depth)
        x = jnp.dot(l, r, preferred_element_type=jnp.float32)
        for h in range(halves):
            part = x[:, h * 128 : (h + 1) * 128]
            cross[h, pl.ds(pl.multiple_of(k * sc, sc), sc), :] = part[:sc]
            cross[h, pl.ds(pl.multiple_of((bins + k) * sc, sc), sc), :] = part[sc:]
        return carry

    lax.fori_loop(0, bins, bin_step, 0, unroll=8)

    inv = inv_ref[...]
    per = 128 // slot

    def source_step(s, carry):
        for h in range(halves):
            x = cross[h, pl.ds(s, 2 * bins, stride=sc), :]
            x = x * scale_ref[s][:, h * 128 : (h + 1) * 128]
            y = lax.dot_general(
                x.astype(jnp.bfloat16),
                inv,
                (((0,), (0,)), ((), ())),
                preferred_element_type=jnp.float32,
            )
            out_ref[s, h * per : (h + 1) * per, 0] = y.reshape(per, slot, LAGS)
        return carry

    lax.fori_loop(0, sc, source_step, 0, unroll=4)


def pair_block(src, recv, scale, inverse, slot):
    bins, _, sources, depth = src.shape
    receivers = recv.shape[2]
    sc = min(64, sources)
    ti = min(256, receivers)
    return pl.pallas_call(
        pair_kernel,
        grid=(receivers // ti, sources // sc),
        in_specs=[
            pl.BlockSpec((bins, 2, sc, depth), lambda i, s: (0, 0, s, 0)),
            pl.BlockSpec((bins, depth, ti), lambda i, s: (0, 0, i)),
            pl.BlockSpec((sc, 1, ti), lambda i, s: (s, 0, i)),
            pl.BlockSpec((2 * bins, LAGS), lambda i, s: (0, 0)),
        ],
        out_specs=pl.BlockSpec(
            (sc, ti // slot, 1, slot, LAGS), lambda i, s: (s, i, 0, 0, 0)
        ),
        out_shape=jax.ShapeDtypeStruct(
            (sources, receivers // slot, 1, slot, LAGS), jnp.float32
        ),
        scratch_shapes=[pltpu.VMEM((ti // 128, 2 * bins * sc, 128), jnp.float32)],
        compiler_params=pltpu.CompilerParams(vmem_limit_bytes=58 * 1024 * 1024),
        cost_estimate=pl.CostEstimate(
            flops=2 * sources * receivers * 2 * bins * (depth + LAGS),
            bytes_accessed=sources * receivers * LAGS * 4,
            transcendentals=0,
        ),
        name="pairs",
    )(src, recv, scale[:, None, :], inverse)


def on_device(series, validity):
    win_rows, channels, samples = series.shape
    taper, inverse = build_tables(samples)
    spectra = jnp.dot(
        series.reshape(win_rows * channels, samples),
        jnp.asarray(taper),
        preferred_element_type=jnp.float32,
    ).reshape(win_rows, channels, 2 * BINS)
    energy = jnp.mean(spectra * spectra, axis=-1, keepdims=True)
    flag_float = validity.astype(jnp.float32)
    whitened = (spectra * lax.rsqrt(energy + 1e-06) * flag_float[..., None]).astype(jnp.bfloat16)
    flags = validity.astype(jnp.bfloat16)

    blocks = lax.axis_size("chan")
    slots = lax.axis_size("win")
    slot = channels // slots
    v = lax.axis_index("win")

    local = whitened.reshape(win_rows, channels, 2, BINS).transpose(3, 2, 0, 1)
    local = local.reshape(BINS, 2 * win_rows, channels)
    src = lax.all_gather(local, "win", axis=1, tiled=True)
    depth = src.shape[1]
    own = lax.dynamic_slice_in_dim(src, v * slot, slot, axis=2)
    recv = lax.all_gather(own, "chan", axis=0)
    src_flags = lax.all_gather(flags, "win", axis=0, tiled=True)
    own_flags = lax.dynamic_slice_in_dim(src_flags, v * slot, slot, axis=1)
    recv_flags = lax.all_gather(own_flags, "chan", axis=1, tiled=True)
    count = jnp.einsum("ws,wi->si", src_flags, recv_flags, preferred_element_type=jnp.float32)
    scale = 1.0 / jnp.maximum(count, 1.0)

    parts = src.reshape(BINS, slots, 2, win_rows, channels)
    turned = jnp.concatenate([-parts[:, :, 1:], parts[:, :, :1]], axis=2)
    both = jnp.stack([src, turned.reshape(BINS, depth, channels)], axis=1)
    src_l = jnp.swapaxes(both, 2, 3)
    recv_r = jnp.transpose(recv, (1, 2, 0, 3)).reshape(BINS, depth, blocks * slot)
    return pair_block(src_l, recv_r, scale, jnp.asarray(inverse), slot)


def solution(mesh):
    return jax.shard_map(
        on_device,
        mesh=mesh,
        in_specs=(P("win", "chan", None), P("win", "chan")),
        out_specs=P("chan", None, "win", None, None),
        check_vma=False,
    )
```
